32 devices in a mesh: mode: 4 (over z), space: 8 (over y, x, core).
Axes of the slice: x: 2, y: 2, z: 4, core: 2. Of those that a mesh axis runs over, the one named last changes fastest.
Arguments:
- traces: float32 [120, 24576], P('mode', 'space'), may hold values from -6 to 6
- elem_mats: float32 [5, 36, 8192], P(None, None, 'space'), may hold values from -1.8 to 1.8
- face_links: int32 [6, 8192], P(None, 'space'), may hold values from 0 to 4095
- pair_modes: int32 [2, 1440], replicated, may hold values from 0 to 119
- pair_terms: int32 [1440], replicated, may hold values from 0 to 3
- pair_values: float32 [1440], replicated, may hold values from -3 to 3
Outputs:
- applied: float32 [120, 24576], P('mode', 'space')
The draws below stay inside these ranges and needn't reach their ends.
Inputs may be any that keep to these rules, and one draw needn't show every extreme that they name: `face_links`: indices into an element's subdomain's 3072 faces preceded and followed by 512 faces of the neighbouring subdomains.
All inputs are finite; a program needn't handle non-finite values.
Results may differ from the reference program's by a relative error of at most 0.0001.
Values sent between devices are 32-bit elements; how exact they have to be, the bound alone decides.
A program may use at most 128 MiB of HBM per device.

```python
import jax
import jax.numpy as jnp
from jax import lax

MODES = 120
KL = 4
E_DEV = 1024
F_DEV = 3072
HALO = 512
ELEMS = 8192
FACES = 24576
NNZ = 1440


def plant(array, key, least, largest):
    longest = array.shape.index(max(array.shape))
    spots = []
    for shift in (0, 1):
        where = [jax.random.randint(jax.random.fold_in(key, axis), (), 0, length) for axis, length in enumerate(array.shape)]
        where[longest] = (where[longest] + shift) % array.shape[longest]
        spots.append(tuple(where))
    return array.at[spots[0]].set(least).at[spots[1]].set(largest)


def shard_levels(stream_key, extent, cuts, smallest, high):
    gain, own = 1.0, jax.random.fold_in(stream_key, 6)
    for position, shards_of in cuts:
        draws = jnp.exp(jax.random.uniform(jax.random.fold_in(own, position), (shards_of,), jnp.float32, smallest / len(cuts), high / len(cuts)))
        gain = gain * jnp.repeat(draws, extent[position] // shards_of).reshape([-1 if axis == position else 1 for axis in range(len(extent))])
    return gain


def gaussian(own_key, extent, spread, most, split=(), kind=jnp.bfloat16):
    array = spread * jax.random.normal(own_key, extent, jnp.float32)
    if split:
        array = array * shard_levels(own_key, extent, split, -0.22, 0.18)
    return jnp.clip(array, -most, most).astype(kind)


def setup_inputs(seed: int = 0) -> dict:
    seeds = jax.random.split(jax.random.key(seed), 7)
    return {
        "traces": gaussian(seeds[0], (MODES, FACES), 1.0, 6.0, ((0, 4), (1, 8)), jnp.float32),
        "elem_mats": gaussian(seeds[1], (KL + 1, 36, ELEMS), 0.3, 1.8, ((2, 8),), jnp.float32),
        "face_links": plant(jax.random.randint(seeds[2], (6, ELEMS), 0, F_DEV + 2 * HALO), jax.random.fold_in(seeds[2], 1), 0, (F_DEV + 2 * HALO) - 1).astype(jnp.int32),
        "pair_modes": plant(jax.random.randint(seeds[3], (2, NNZ), 0, MODES), jax.random.fold_in(seeds[3], 1), 0, MODES - 1).astype(jnp.int32),
        "pair_terms": plant(jax.random.randint(seeds[4], (NNZ,), 0, KL), jax.random.fold_in(seeds[4], 1), 0, KL - 1).astype(jnp.int32),
        "pair_values": gaussian(seeds[5], (NNZ,), 0.5, 3.0, (), jnp.float32),
    }


def coupling_table(pair_modes, pair_terms, pair_values, mode_count, term_count):
    coupling = jnp.zeros((term_count + 1, mode_count, mode_count), jnp.float32)
    coupling = coupling.at[pair_terms + 1, pair_modes[0], pair_modes[1]].add(pair_values)
    return coupling.at[0].set(jnp.eye(mode_count, dtype=jnp.float32))


def element_terms(values, links, mats):
    gathered = values[:, links]
    square_mats = mats.reshape(mats.shape[0], 6, 6, mats.shape[-1])
    running = square_mats[:, None, :, 0, :] * gathered[None, :, 0, None, :]
    for column in range(1, 6):
        running = running + square_mats[:, None, :, column, :] * gathered[None, :, column, None, :]
    return running


def assemble(local_terms, links, ext_width):
    flat = local_terms.reshape(local_terms.shape[:-2] + (-1,))
    zeros = jnp.zeros(local_terms.shape[:-2] + (ext_width,), jnp.float32)
    return zeros.at[..., links.reshape(-1)].add(flat)


def reference(traces, elem_mats, face_links, pair_modes, pair_terms, pair_values):
    mode_count = traces.shape[0]
    term_count = elem_mats.shape[0] - 1
    coupling = coupling_table(pair_modes, pair_terms, pair_values, mode_count, term_count)
    padded = jnp.pad(traces, ((0, 0), (HALO, HALO)))
    owner_index = (jnp.arange(ELEMS, dtype=jnp.int32) // E_DEV).astype(jnp.int32)
    global_links = (face_links + (owner_index * F_DEV)[None, :]).astype(jnp.int32)
    ext_width = padded.shape[1]
    result = jnp.zeros(traces.shape, jnp.float32)
    for kl_term in range(term_count + 1):
        local_terms = element_terms(padded, global_links, elem_mats[kl_term:kl_term + 1])[0]
        assembled = assemble(local_terms, global_links, ext_width)[:, HALO:HALO + FACES]
        result = result + jnp.dot(coupling[kl_term], assembled, precision=lax.Precision.HIGHEST)
    return result
```

```python
import functools

import jax
import jax.numpy as jnp
from jax import lax
from jax.experimental import pallas as pl
from jax.experimental.pallas import tpu as pltpu
from jax.sharding import PartitionSpec as P

HALO = 512
DIGIT = 256
BF = jnp.bfloat16


def coupling_rows(pair_modes, pair_terms, pair_values, rows, mode_count, term_count, first, pad_rows, pad_cols):
    groups = mode_count // rows
    row_key = jnp.where(
        (pair_modes[0] >= first) & (pair_modes[0] < first + rows),
        (pair_terms + 1) * pad_rows + pair_modes[0] - first,
        -1,
    )
    col_key = (pair_modes[1] // rows) * pad_cols + pair_modes[1] % rows
    row_ids = jnp.arange((term_count + 1) * pad_rows, dtype=jnp.int32)
    col_ids = jnp.arange(groups * pad_cols, dtype=jnp.int32)
    hits = (row_key[None, :] == row_ids[:, None]).astype(jnp.float32) * pair_values[None, :]
    cols = (col_key[:, None] == col_ids[None, :]).astype(jnp.float32)
    table = jnp.dot(hits, cols, precision=lax.Precision.HIGHEST)
    own = (first // rows) * pad_cols
    unit = (row_ids[:, None] + own == col_ids[None, :]) & (row_ids[:, None] < rows)
    return table + unit.astype(jnp.float32)


def split(value):
    high = value.astype(BF)
    return high, (value - high.astype(jnp.float32)).astype(BF)


def prepare(links_ref, low_ref, slots, elems):
    ids = lax.broadcasted_iota(jnp.int32, (DIGIT, elems), 0)
    for a in range(slots):
        low = links_ref[a : a + 1, :] % DIGIT
        low_ref[:, a * elems : (a + 1) * elems] = (ids == low).astype(jnp.float32).astype(BF)


def gather_shard(x_ref, links_ref, low_ref, g_ref, row, rows, slots, elems, ext):
    tops = ext // DIGIT
    high, low = split(x_ref[...])

    for a in range(slots):
        table = low_ref[:, a * elems : (a + 1) * elems]
        tops_of = links_ref[a : a + 1, :] // DIGIT
        total = jnp.zeros((rows, elems), jnp.float32)
        for h in range(tops):
            at = slice(h * DIGIT, (h + 1) * DIGIT)
            part = jnp.dot(high[:, at], table, preferred_element_type=jnp.float32)
            part = part + jnp.dot(low[:, at], table, preferred_element_type=jnp.float32)
            total = jnp.where(tops_of == h, part, total)
        g_ref[pl.ds(row, rows), a * elems : (a + 1) * elems] = total


def finish(coupling_ref, mats_ref, links_ref, low_ref, g_ref, z_ref, v_ref, acc_ref, terms, pad, slots, elems, ext):
    tops = ext // DIGIT
    c_high, c_low = split(coupling_ref[...])
    for a in range(slots):
        at = slice(a * elems, (a + 1) * elems)
        g_high, g_low = split(g_ref[:, at])
        z = jnp.dot(c_high, g_high, preferred_element_type=jnp.float32)
        z = z + jnp.dot(c_high, g_low, preferred_element_type=jnp.float32)
        z_ref[:, at] = z + jnp.dot(c_low, g_high, preferred_element_type=jnp.float32)
    for e in range(0, elems, 128):
        for a in range(slots):
            total = jnp.zeros((pad, 128), jnp.float32)
            for k in range(terms):
                for b in range(slots):
                    total = total + (
                        mats_ref[k, slots * a + b : slots * a + b + 1, e : e + 128]
                        * z_ref[k * pad : (k + 1) * pad, b * elems + e : b * elems + e + 128]
                    )
            high, low = split(total)
            v_ref[:pad, a * elems + e : a * elems + e + 128] = high
            v_ref[pad:, a * elems + e : a * elems + e + 128] = low
    for a in range(slots):
        at = slice(a * elems, (a + 1) * elems)
        v = v_ref[:, at]
        tops_of = links_ref[a : a + 1, :] // DIGIT
        parts = [v * (tops_of == h).astype(jnp.float32).astype(BF) for h in range(tops)]
        add = lax.dot_general(
            jnp.concatenate(parts, axis=0),
            low_ref[:, at],
            (((1,), (1,)), ((), ())),
            preferred_element_type=jnp.float32,
        )
        if a == 0:
            acc_ref[...] = add
        else:
            acc_ref[...] += add


def kernel(dims, x_ref, coupling_ref, mats_ref, links_ref, out_ref, low_ref, g_ref, z_ref, v_ref, acc_ref):
    groups, rows, pad, terms, slots, elems, ext = dims
    prepare(links_ref, low_ref, slots, elems)
    g_ref[...] = jnp.zeros_like(g_ref)
    for d in range(groups):
        gather_shard(x_ref.at[d], links_ref, low_ref, g_ref, d * pad, rows, slots, elems, ext)
    finish(coupling_ref, mats_ref, links_ref, low_ref, g_ref, z_ref, v_ref, acc_ref, terms, pad, slots, elems, ext)
    for h in range(ext // DIGIT):
        base = 2 * pad * h
        total = acc_ref[base : base + pad, :] + acc_ref[base + pad : base + 2 * pad, :]
        out_ref[:, h * DIGIT : (h + 1) * DIGIT] = total[:rows]


def body(traces, elem_mats, face_links, pair_modes, pair_terms, pair_values):
    rows, faces = traces.shape
    terms = elem_mats.shape[0]
    slots, elems = face_links.shape
    groups, spaces = lax.axis_size("mode"), lax.axis_size("space")
    ext = faces + 2 * HALO
    pad = -(-rows // 8) * 8
    first = lax.axis_index("mode") * rows
    coupling = coupling_rows(
        pair_modes, pair_terms, pair_values, rows, rows * groups, terms - 1, first, pad, pad
    )
    up = [(i, i + 1) for i in range(spaces - 1)]
    down = [(i + 1, i) for i in range(spaces - 1)]
    before = lax.ppermute(traces[:, faces - HALO :], "space", up)
    after = lax.ppermute(traces[:, :HALO], "space", down)
    extended = jnp.concatenate([before, traces, after], axis=1)
    x = lax.all_gather(extended, "mode")
    dims = (groups, rows, pad, terms, slots, elems, ext)
    tops = ext // DIGIT
    vmem = pl.BlockSpec(memory_space=pltpu.VMEM)
    out = pl.pallas_call(
        functools.partial(kernel, dims),
        out_shape=jax.ShapeDtypeStruct((rows, ext), jnp.float32),
        in_specs=[vmem] * 4,
        out_specs=vmem,
        scratch_shapes=[
            pltpu.VMEM((DIGIT, slots * elems), BF),
            pltpu.VMEM((groups * pad, slots * elems), jnp.float32),
            pltpu.VMEM((terms * pad, slots * elems), jnp.float32),
            pltpu.VMEM((2 * pad, slots * elems), BF),
            pltpu.VMEM((2 * pad * tops, DIGIT), jnp.float32),
        ],
        compiler_params=pltpu.CompilerParams(vmem_limit_bytes=48 * 1024 * 1024),
    )(x, coupling, elem_mats, face_links)
    from_next = lax.ppermute(out[:, :HALO], "space", down)
    from_prev = lax.ppermute(out[:, HALO + faces :], "space", up)
    mid = out[:, HALO : HALO + faces]
    return jnp.concatenate(
        [mid[:, :HALO] + from_prev, mid[:, HALO : faces - HALO], mid[:, faces - HALO :] + from_next], axis=1
    )


def solution(mesh):
    return jax.shard_map(
        body,
        mesh=mesh,
        in_specs=(P("mode", "space"), P(None, None, "space"), P(None, "space"), P(), P(), P()),
        out_specs=P("mode", "space"),
        check_vma=False,
    )
```

```python
import functools

import jax
import jax.numpy as jnp
from jax import lax
from jax.experimental import pallas as pl
from jax.experimental.pallas import tpu as pltpu
from jax.sharding import PartitionSpec as P

HALO = 512
DIGIT = 256
BF = jnp.bfloat16


def coupling_rows(pair_modes, pair_terms, pair_values, rows, mode_count, term_count, first, pad_rows, pad_cols):
    groups = mode_count // rows
    row_key = jnp.where(
        (pair_modes[0] >= first) & (pair_modes[0] < first + rows),
        (pair_terms + 1) * pad_rows + pair_modes[0] - first,
        -1,
    )
    col_key = (pair_modes[1] // rows) * pad_cols + pair_modes[1] % rows
    row_ids = jnp.arange((term_count + 1) * pad_rows, dtype=jnp.int32)
    col_ids = jnp.arange(groups * pad_cols, dtype=jnp.int32)
    hits = (row_key[None, :] == row_ids[:, None]).astype(jnp.float32) * pair_values[None, :]
    cols = (col_key[:, None] == col_ids[None, :]).astype(jnp.float32)
    table = jnp.dot(hits, cols, precision=lax.Precision.HIGHEST)
    own = (first // rows) * pad_cols
    unit = (row_ids[:, None] + own == col_ids[None, :]) & (row_ids[:, None] < rows)
    return table + unit.astype(jnp.float32)


def split(value):
    high = value.astype(BF)
    return high, (value - high.astype(jnp.float32)).astype(BF)


def kernel(dims, x_ref, coupling_ref, mats_ref, links_ref, out_ref, low_ref, x2_ref, z_ref, v_ref, acc_ref):
    groups, rows, pad, terms, slots, elems, ext = dims
    tops = ext // DIGIT
    per_slot = elems // DIGIT
    chunks = slots * per_slot
    modes = groups * pad
    x2_ref[...] = jnp.zeros_like(x2_ref)
    for d in range(groups):
        for h in range(tops):
            high, low = split(x_ref[d, :, h * DIGIT : (h + 1) * DIGIT])
            base = h * modes + d * pad
            x2_ref[0, base : base + rows, :] = high
            x2_ref[1, base : base + rows, :] = low
    c_high, c_low = split(coupling_ref[...])

    @pl.loop(0, chunks)
    def _(c):
        links = links_ref[c]
        ids = lax.broadcasted_iota(jnp.int32, (DIGIT, DIGIT), 0)
        table = (ids == links % DIGIT).astype(jnp.float32).astype(BF)
        low_ref[c] = table
        found = jnp.dot(x2_ref[0], table, preferred_element_type=jnp.float32)
        found = found + jnp.dot(x2_ref[1], table, preferred_element_type=jnp.float32)
        tops_of = links // DIGIT
        g = jnp.zeros((modes, DIGIT), jnp.float32)
        for h in range(tops):
            g = jnp.where(tops_of == h, found[h * modes : (h + 1) * modes], g)
        g_high, g_low = split(g)
        z = jnp.dot(c_high, g_high, preferred_element_type=jnp.float32)
        z = z + jnp.dot(c_high, g_low, preferred_element_type=jnp.float32)
        z_ref[c] = z + jnp.dot(c_low, g_high, preferred_element_type=jnp.float32)

    acc_ref[...] = jnp.zeros_like(acc_ref)

    @pl.loop(0, slots)
    def _(a):
        for e in range(0, elems, 128):
            q, lane = e // DIGIT, e % DIGIT
            total = jnp.zeros((pad, 128), jnp.float32)
            for k in range(terms):
                for b in range(slots):
                    total = total + (
                        mats_ref[k, a, b : b + 1, e : e + 128]
                        * z_ref[b * per_slot + q, k * pad : (k + 1) * pad, lane : lane + 128]
                    )
            high, low = split(total)
            v_ref[a * per_slot + q, :pad, lane : lane + 128] = high
            v_ref[a * per_slot + q, pad:, lane : lane + 128] = low

    @pl.loop(0, chunks)
    def _(c):
        v = v_ref[c]
        tops_of = links_ref[c] // DIGIT
        parts = [v * (tops_of == h).astype(jnp.float32).astype(BF) for h in range(tops)]
        acc_ref[...] += lax.dot_general(
            jnp.concatenate(parts, axis=0),
            low_ref[c],
            (((1,), (1,)), ((), ())),
            preferred_element_type=jnp.float32,
        )

    for h in range(tops):
        base = 2 * pad * h
        total = acc_ref[base : base + pad, :] + acc_ref[base + pad : base + 2 * pad, :]
        out_ref[:, h * DIGIT : (h + 1) * DIGIT] = total[:rows]


def body(traces, elem_mats, face_links, pair_modes, pair_terms, pair_values):
    rows, faces = traces.shape
    terms = elem_mats.shape[0]
    slots, elems = face_links.shape
    groups, spaces = lax.axis_size("mode"), lax.axis_size("space")
    ext = faces + 2 * HALO
    pad = -(-rows // 16) * 16
    first = lax.axis_index("mode") * rows
    coupling = coupling_rows(
        pair_modes, pair_terms, pair_values, rows, rows * groups, terms - 1, first, pad, pad
    )
    up = [(i, i + 1) for i in range(spaces - 1)]
    down = [(i + 1, i) for i in range(spaces - 1)]
    before = lax.ppermute(traces[:, faces - HALO :], "space", up)
    after = lax.ppermute(traces[:, :HALO], "space", down)
    extended = jnp.concatenate([before, traces, after], axis=1)
    x = lax.all_gather(extended, "mode")
    dims = (groups, rows, pad, terms, slots, elems, ext)
    tops = ext // DIGIT
    chunks = slots * elems // DIGIT
    vmem = pl.BlockSpec(memory_space=pltpu.VMEM)
    out = pl.pallas_call(
        functools.partial(kernel, dims),
        out_shape=jax.ShapeDtypeStruct((rows, ext), jnp.float32),
        in_specs=[vmem] * 4,
        out_specs=vmem,
        scratch_shapes=[
            pltpu.VMEM((chunks, DIGIT, DIGIT), BF),
            pltpu.VMEM((2, tops * groups * pad, DIGIT), BF),
            pltpu.VMEM((chunks, terms * pad, DIGIT), jnp.float32),
            pltpu.VMEM((chunks, 2 * pad, DIGIT), BF),
            pltpu.VMEM((2 * pad * tops, DIGIT), jnp.float32),
        ],
        compiler_params=pltpu.CompilerParams(vmem_limit_bytes=48 * 1024 * 1024),
    )(x, coupling, elem_mats.reshape(terms, slots, slots, elems), face_links.reshape(chunks, 1, DIGIT))
    from_next = lax.ppermute(out[:, :HALO], "space", down)
    from_prev = lax.ppermute(out[:, HALO + faces :], "space", up)
    mid = out[:, HALO : HALO + faces]
    return jnp.concatenate(
        [mid[:, :HALO] + from_prev, mid[:, HALO : faces - HALO], mid[:, faces - HALO :] + from_next], axis=1
    )


def solution(mesh):
    return jax.shard_map(
        body,
        mesh=mesh,
        in_specs=(P("mode", "space"), P(None, None, "space"), P(None, "space"), P(), P(), P()),
        out_specs=P("mode", "space"),
        check_vma=False,
    )
```

```python
import functools

import jax
import jax.numpy as jnp
from jax import lax
from jax.experimental import pallas as pl
from jax.experimental.pallas import tpu as pltpu
from jax.sharding import PartitionSpec as P

HALO = 512
DIGIT = 256
BF = jnp.bfloat16


def coupling_rows(pair_modes, pair_terms, pair_values, rows, mode_count, term_count, first, pad_rows, pad_cols):
    groups = mode_count // rows
    row_key = jnp.where(
        (pair_modes[0] >= first) & (pair_modes[0] < first + rows),
        (pair_terms + 1) * pad_rows + pair_modes[0] - first,
        -1,
    )
    col_key = ((pair_modes[1] // rows - first // rows + groups) % groups) * pad_cols + pair_modes[1] % rows
    row_ids = jnp.arange((term_count + 1) * pad_rows, dtype=jnp.int32)
    col_ids = jnp.arange(groups * pad_cols, dtype=jnp.int32)
    hits = (row_key[None, :] == row_ids[:, None]).astype(jnp.float32) * pair_values[None, :]
    cols = (col_key[:, None] == col_ids[None, :]).astype(jnp.float32)
    table = jnp.dot(hits, cols, precision=lax.Precision.HIGHEST)
    unit = (row_ids[:, None] == col_ids[None, :]) & (row_ids[:, None] < rows)
    return table + unit.astype(jnp.float32)


def split(value):
    high = value.astype(BF)
    return high, (value - high.astype(jnp.float32)).astype(BF)


def kernel(dims, own_ref, *refs):
    groups = dims[0]
    lower, upper = refs[: groups - 1], refs[groups - 1 : 2 * groups - 2]
    compute(dims, own_ref, lower, upper, *refs[2 * groups - 2 :])


def compute(dims, own_ref, lower, upper, coupling_ref, mats_ref, links_ref, out_ref, low_ref, x2_ref, z_ref, v_ref, acc_ref):
    groups, rows, pad, terms, slots, elems, ext = dims
    tops = ext // DIGIT
    per_slot = elems // DIGIT
    chunks = slots * per_slot
    modes = groups * pad
    x2_ref[...] = jnp.zeros_like(x2_ref)
    for d in range(groups):
        for h in range(tops):
            at = slice(h * DIGIT, (h + 1) * DIGIT)
            block = own_ref[:, at] if d == 0 else upper[d - 1][:, at] + lower[groups - d - 1][:, at]
            high, low = split(block)
            base = h * modes + d * pad
            x2_ref[0, base : base + rows, :] = high
            x2_ref[1, base : base + rows, :] = low
    c_high, c_low = split(coupling_ref[...])

    @pl.loop(0, chunks)
    def _(c):
        links = links_ref[c]
        ids = lax.broadcasted_iota(jnp.int32, (DIGIT, DIGIT), 0)
        table = (ids == links % DIGIT).astype(jnp.float32).astype(BF)
        low_ref[c] = table
        found = jnp.dot(x2_ref[0], table, preferred_element_type=jnp.float32)
        found = found + jnp.dot(x2_ref[1], table, preferred_element_type=jnp.float32)
        tops_of = links // DIGIT
        g = jnp.zeros((modes, DIGIT), jnp.float32)
        for h in range(tops):
            g = jnp.where(tops_of == h, found[h * modes : (h + 1) * modes], g)
        g_high, g_low = split(g)
        z = jnp.dot(c_high, g_high, preferred_element_type=jnp.float32)
        z = z + jnp.dot(c_high, g_low, preferred_element_type=jnp.float32)
        z_ref[c] = z + jnp.dot(c_low, g_high, preferred_element_type=jnp.float32)

    acc_ref[...] = jnp.zeros_like(acc_ref)

    @pl.loop(0, slots)
    def _(a):
        for e in range(0, elems, 128):
            q, lane = e // DIGIT, e % DIGIT
            total = jnp.zeros((pad, 128), jnp.float32)
            for k in range(terms):
                for b in range(slots):
                    total = total + (
                        mats_ref[k, a, b : b + 1, e : e + 128]
                        * z_ref[b * per_slot + q, k * pad : (k + 1) * pad, lane : lane + 128]
                    )
            high, low = split(total)
            v_ref[a * per_slot + q, :pad, lane : lane + 128] = high
            v_ref[a * per_slot + q, pad:, lane : lane + 128] = low

    @pl.loop(0, chunks)
    def _(c):
        v = v_ref[c]
        tops_of = links_ref[c] // DIGIT
        parts = [v * (tops_of == h).astype(jnp.float32).astype(BF) for h in range(tops)]
        acc_ref[...] += lax.dot_general(
            jnp.concatenate(parts, axis=0),
            low_ref[c],
            (((1,), (1,)), ((), ())),
            preferred_element_type=jnp.float32,
        )

    for h in range(tops):
        base = 2 * pad * h
        total = acc_ref[base : base + pad, :] + acc_ref[base + pad : base + 2 * pad, :]
        out_ref[:, h * DIGIT : (h + 1) * DIGIT] = total[:rows]


def body(traces, elem_mats, face_links, pair_modes, pair_terms, pair_values):
    rows, faces = traces.shape
    terms = elem_mats.shape[0]
    slots, elems = face_links.shape
    groups, spaces = lax.axis_size("mode"), lax.axis_size("space")
    ext = faces + 2 * HALO
    pad = -(-rows // 16) * 16
    first = lax.axis_index("mode") * rows
    coupling = coupling_rows(
        pair_modes, pair_terms, pair_values, rows, rows * groups, terms - 1, first, pad, pad
    )
    up = [(i, i + 1) for i in range(spaces - 1)]
    down = [(i + 1, i) for i in range(spaces - 1)]
    before = lax.ppermute(traces[:, faces - HALO :], "space", up)
    after = lax.ppermute(traces[:, :HALO], "space", down)
    extended = jnp.concatenate([before, traces, after], axis=1)
    lower, upper = [extended], [extended]
    right = [(i, i + 1) for i in range(groups - 1)]
    left = [(i + 1, i) for i in range(groups - 1)]
    for _ in range(groups - 1):
        lower.append(lax.ppermute(lower[-1], "mode", right))
        upper.append(lax.ppermute(upper[-1], "mode", left))
    dims = (groups, rows, pad, terms, slots, elems, ext)
    tops = ext // DIGIT
    chunks = slots * elems // DIGIT
    vmem = pl.BlockSpec(memory_space=pltpu.VMEM)
    out = pl.pallas_call(
        functools.partial(kernel, dims),
        out_shape=jax.ShapeDtypeStruct((rows, ext), jnp.float32),
        in_specs=[vmem] * (2 * groups + 2),
        out_specs=vmem,
        scratch_shapes=[
            pltpu.VMEM((chunks, DIGIT, DIGIT), BF),
            pltpu.VMEM((2, tops * groups * pad, DIGIT), BF),
            pltpu.VMEM((chunks, terms * pad, DIGIT), jnp.float32),
            pltpu.VMEM((chunks, 2 * pad, DIGIT), BF),
            pltpu.VMEM((2 * pad * tops, DIGIT), jnp.float32),
        ],
        compiler_params=pltpu.CompilerParams(vmem_limit_bytes=48 * 1024 * 1024),
    )(extended, *lower[1:], *upper[1:], coupling, elem_mats.reshape(terms, slots, slots, elems), face_links.reshape(chunks, 1, DIGIT))
    from_next = lax.ppermute(out[:, :HALO], "space", down)
    from_prev = lax.ppermute(out[:, HALO + faces :], "space", up)
    mid = out[:, HALO : HALO + faces]
    return jnp.concatenate(
        [mid[:, :HALO] + from_prev, mid[:, HALO : faces - HALO], mid[:, faces - HALO :] + from_next], axis=1
    )


def solution(mesh):
    return jax.shard_map(
        body,
        mesh=mesh,
        in_specs=(P("mode", "space"), P(None, None, "space"), P(None, "space"), P(), P(), P()),
        out_specs=P("mode", "space"),
        check_vma=False,
    )
```

```python
import functools

import jax
import jax.numpy as jnp
from jax import lax
from jax.experimental import pallas as pl
from jax.experimental.pallas import tpu as pltpu
from jax.sharding import PartitionSpec as P

HALO = 512
DIGIT = 256
BF = jnp.bfloat16


def coupling_rows(pair_modes, pair_terms, pair_values, rows, mode_count, term_count, first, pad_rows, pad_cols):
    groups = mode_count // rows
    row_key = jnp.where(
        (pair_modes[0] >= first) & (pair_modes[0] < first + rows),
        (pair_terms + 1) * pad_rows + pair_modes[0] - first,
        -1,
    )
    col_key = ((pair_modes[1] // rows - first // rows + groups) % groups) * pad_cols + pair_modes[1] % rows
    row_ids = jnp.arange((term_count + 1) * pad_rows, dtype=jnp.int32)
    col_ids = jnp.arange(groups * pad_cols, dtype=jnp.int32)
    hits = (row_key[None, :] == row_ids[:, None]).astype(jnp.float32) * pair_values[None, :]
    cols = (col_key[:, None] == col_ids[None, :]).astype(jnp.float32)
    table = jnp.dot(hits, cols, precision=lax.Precision.HIGHEST)
    unit = (row_ids[:, None] == col_ids[None, :]) & (row_ids[:, None] < rows)
    return table + unit.astype(jnp.float32)


def split(value):
    high = value.astype(BF)
    return high, (value - high.astype(jnp.float32)).astype(BF)


def digit_table(links):
    ids = lax.broadcasted_iota(jnp.int32, (DIGIT, DIGIT), 0)
    return (ids == links % DIGIT).astype(jnp.float32).astype(BF)


def gather_kernel(dims, *refs):
    groups, rows, pad, terms, slots, elems, ext = dims
    *shards, links_ref, g_ref, x2_ref = refs
    tops = ext // DIGIT
    modes = len(shards) * pad
    x2_ref[...] = jnp.zeros_like(x2_ref)
    for d, shard in enumerate(shards):
        for h in range(tops):
            high, low = split(shard[:, h * DIGIT : (h + 1) * DIGIT])
            base = h * modes + d * pad
            x2_ref[0, base : base + rows, :] = high
            x2_ref[1, base : base + rows, :] = low

    @pl.loop(0, slots * elems // DIGIT)
    def _(c):
        links = links_ref[c]
        table = digit_table(links)
        found = jnp.dot(x2_ref[0], table, preferred_element_type=jnp.float32)
        found = found + jnp.dot(x2_ref[1], table, preferred_element_type=jnp.float32)
        tops_of = links // DIGIT
        g = jnp.zeros((modes, DIGIT), jnp.float32)
        for h in range(tops):
            g = jnp.where(tops_of == h, found[h * modes : (h + 1) * modes], g)
        g_ref[c] = g


def gather(dims, shards, links):
    groups, rows, pad, terms, slots, elems, ext = dims
    chunks, modes, tops = links.shape[0], len(shards) * pad, ext // DIGIT
    vmem = pl.BlockSpec(memory_space=pltpu.VMEM)
    return pl.pallas_call(
        functools.partial(gather_kernel, dims),
        out_shape=jax.ShapeDtypeStruct((chunks, modes, DIGIT), jnp.float32),
        in_specs=[vmem] * (len(shards) + 1),
        out_specs=vmem,
        scratch_shapes=[pltpu.VMEM((2, tops * modes, DIGIT), BF)],
        cost_estimate=pl.CostEstimate(
            flops=16 * tops * modes * DIGIT * chunks * DIGIT,
            bytes_accessed=4 * modes * (ext + chunks * DIGIT),
            transcendentals=0,
        ),
        compiler_params=pltpu.CompilerParams(vmem_limit_bytes=24 * 1024 * 1024),
    )(*shards, links)


def kernel(dims, *refs):
    groups = dims[0]
    compute(dims, refs[0], refs[1:groups], *refs[groups:])


def compute(dims, own_ref, step_refs, coupling_ref, mats_ref, links_ref, out_ref, z_ref, v_ref, acc_ref):
    groups, rows, pad, terms, slots, elems, ext = dims
    tops = ext // DIGIT
    per_slot = elems // DIGIT
    chunks = slots * per_slot
    c_high, c_low = split(coupling_ref[...])

    @pl.loop(0, chunks)
    def _(c):
        blocks = [own_ref[c]] + [
            step_refs[d - 1][c, pad:, :] + step_refs[groups - d - 1][c, :pad, :] for d in range(1, groups)
        ]
        g_high, g_low = split(jnp.concatenate(blocks, axis=0))
        z = jnp.dot(c_high, g_high, preferred_element_type=jnp.float32)
        z = z + jnp.dot(c_high, g_low, preferred_element_type=jnp.float32)
        z_ref[c] = z + jnp.dot(c_low, g_high, preferred_element_type=jnp.float32)

    acc_ref[...] = jnp.zeros_like(acc_ref)

    @pl.loop(0, slots)
    def _(a):
        for e in range(0, elems, 128):
            q, lane = e // DIGIT, e % DIGIT
            total = jnp.zeros((pad, 128), jnp.float32)
            for k in range(terms):
                for b in range(slots):
                    total = total + (
                        mats_ref[k, a, b : b + 1, e : e + 128]
                        * z_ref[b * per_slot + q, k * pad : (k + 1) * pad, lane : lane + 128]
                    )
            high, low = split(total)
            v_ref[a * per_slot + q, :pad, lane : lane + 128] = high
            v_ref[a * per_slot + q, pad:, lane : lane + 128] = low

    @pl.loop(0, chunks)
    def _(c):
        v = v_ref[c]
        tops_of = links_ref[c] // DIGIT
        parts = [v * (tops_of == h).astype(jnp.float32).astype(BF) for h in range(tops)]
        acc_ref[...] += lax.dot_general(
            jnp.concatenate(parts, axis=0),
            digit_table(links_ref[c]),
            (((1,), (1,)), ((), ())),
            preferred_element_type=jnp.float32,
        )

    for h in range(tops):
        base = 2 * pad * h
        total = acc_ref[base : base + pad, :] + acc_ref[base + pad : base + 2 * pad, :]
        out_ref[:, h * DIGIT : (h + 1) * DIGIT] = total[:rows]


def body(traces, elem_mats, face_links, pair_modes, pair_terms, pair_values):
    rows, faces = traces.shape
    terms = elem_mats.shape[0]
    slots, elems = face_links.shape
    groups, spaces = lax.axis_size("mode"), lax.axis_size("space")
    ext = faces + 2 * HALO
    pad = -(-rows // 16) * 16
    first = lax.axis_index("mode") * rows
    coupling = coupling_rows(
        pair_modes, pair_terms, pair_values, rows, rows * groups, terms - 1, first, pad, pad
    )
    up = [(i, i + 1) for i in range(spaces - 1)]
    down = [(i + 1, i) for i in range(spaces - 1)]
    before = lax.ppermute(traces[:, faces - HALO :], "space", up)
    after = lax.ppermute(traces[:, :HALO], "space", down)
    extended = jnp.concatenate([before, traces, after], axis=1)
    lower, upper = [extended], [extended]
    right = [(i, i + 1) for i in range(groups - 1)]
    left = [(i + 1, i) for i in range(groups - 1)]
    for _ in range(groups - 1):
        lower.append(lax.ppermute(lower[-1], "mode", right))
        upper.append(lax.ppermute(upper[-1], "mode", left))
    dims = (groups, rows, pad, terms, slots, elems, ext)
    tops = ext // DIGIT
    chunks = slots * elems // DIGIT
    links = face_links.reshape(chunks, 1, DIGIT)
    own = gather(dims, [extended], links)
    steps = [gather(dims, [lower[r], upper[r]], links) for r in range(1, groups)]
    vmem = pl.BlockSpec(memory_space=pltpu.VMEM)
    out = pl.pallas_call(
        functools.partial(kernel, dims),
        out_shape=jax.ShapeDtypeStruct((rows, ext), jnp.float32),
        in_specs=[vmem] * (groups + 3),
        out_specs=vmem,
        scratch_shapes=[
            pltpu.VMEM((chunks, terms * pad, DIGIT), jnp.float32),
            pltpu.VMEM((chunks, 2 * pad, DIGIT), BF),
            pltpu.VMEM((2 * pad * tops, DIGIT), jnp.float32),
        ],
        compiler_params=pltpu.CompilerParams(vmem_limit_bytes=48 * 1024 * 1024),
    )(own, *steps, coupling, elem_mats.reshape(terms, slots, slots, elems), links)
    from_next = lax.ppermute(out[:, :HALO], "space", down)
    from_prev = lax.ppermute(out[:, HALO + faces :], "space", up)
    mid = out[:, HALO : HALO + faces]
    return jnp.concatenate(
        [mid[:, :HALO] + from_prev, mid[:, HALO : faces - HALO], mid[:, faces - HALO :] + from_next], axis=1
    )


def solution(mesh):
    return jax.shard_map(
        body,
        mesh=mesh,
        in_specs=(P("mode", "space"), P(None, None, "space"), P(None, "space"), P(), P(), P()),
        out_specs=P("mode", "space"),
        check_vma=False,
    )
```
